256 devices in a mesh: rows: 64 (over y, z, core), rhs: 4 (over x).
Axes of the slice: x: 4, y: 4, z: 8, core: 2. Of those that a mesh axis runs over, the one named last changes fastest.
Arguments:
- right_side: bfloat16 [16, 64, 256, 128], P(None, 'rows', 'rhs'), may hold values from -6 to 6
- lower: bfloat16 [16, 64, 4, 128, 128], P(None, 'rows', 'rhs'), may hold values from -0.1875 to 0.1875
- diag_inv: bfloat16 [16, 64, 128, 128], P(None, 'rows'), may hold values from -0.5 to 0.5
- levels: int32 [16, 64], replicated, may hold values from 0 to 7, as said below
- columns: int32 [16, 64, 4], P(None, 'rows'), may hold values from -1 to 1023, as said below
Outputs:
- solved: bfloat16 [16, 64, 256, 128], P(None, 'rows', 'rhs')
The draws below stay inside these ranges and needn't reach their ends.
Inputs may be any that keep to these rules, and one draw needn't show every extreme that they name: `levels`: every index of rows holds exactly 2 block rows of each level. `columns`: level 0 block rows hold only -1. A block row of level l > 0 holds no -1; its slot 0 names a block row of level l - 1, the other slots block rows of levels below l. The stored blocks of one index's block rows of one level name block rows of any one index of rows at most 1 times, and exactly 1 times for some index.
All inputs are finite; a program needn't handle non-finite values.
Results may differ from the reference program's by a relative error of at most 0.0085.
Values may be sent and summed in bfloat16 or wider, within the bound.
No kernel may reach another device: no remote copies, remote signals or barrier semaphores. Data moves between devices by JAX's collectives and lax.ppermute only.
A program may use at most 64 MiB of HBM per device.

```python
import jax
import jax.numpy as jnp

BS = 128
NRHS = 256
NNZ = 4
LEVELS = 8
R_DEV = 16
NB = 1024
N_ROWS = 64


def shared_perms(key):
    count = NB // R_DEV
    keys = jax.random.split(key, count)
    return jax.vmap(lambda k: jax.random.permutation(k, R_DEV))(keys).astype(jnp.int32)


def draw_levels(key, part):
    perms = shared_perms(key)
    return (perms % LEVELS).T.astype(jnp.int32)


def draw_columns(key, part):
    perms = shared_perms(key)
    key = jax.random.fold_in(key, 23)
    count = NB // R_DEV
    each = R_DEV // LEVELS
    inverse = jnp.argsort(perms, axis=1).astype(jnp.int32)
    level_of = (perms % LEVELS).T.astype(jnp.int32)
    own_member = (perms // LEVELS).T.astype(jnp.int32)
    first, second, third = jax.random.split(key, 3)
    shape = (R_DEV, count, NNZ)
    upper = jnp.broadcast_to(jnp.maximum(level_of, 1)[:, :, None], shape)
    chosen = jax.random.randint(first, shape, 0, upper)
    slot = jnp.arange(NNZ, dtype=jnp.int32)[None, None, :]
    target = jnp.where(slot == 0, level_of[:, :, None] - 1, chosen)
    target = jnp.maximum(target, 0)
    spread_keys = jax.random.split(second, count * LEVELS)
    spread = jax.vmap(lambda k: jax.random.permutation(k, count))(spread_keys).astype(jnp.int32)
    spread = spread.reshape(count, LEVELS, count)
    position = (own_member[:, :, None] * NNZ + slot) % count
    holder = jnp.arange(count, dtype=jnp.int32)[None, :, None]
    device = spread[holder, level_of[:, :, None], position]
    member = jax.random.randint(third, shape, 0, each)
    row_local = inverse[device, target + LEVELS * member]
    index = row_local * count + device
    return jnp.where(level_of[:, :, None] == 0, -1, index).astype(jnp.int32)


def block_scale(key, shape, cuts, smallest, top_value):
    def one(dim, blocks):
        draws = jax.random.uniform(jax.random.fold_in(jax.random.fold_in(key, 6), dim), (blocks,), jnp.float32, smallest / len(cuts), top_value / len(cuts))
        return jnp.repeat(jnp.exp(draws), shape[dim] // blocks).reshape((-1,) + (1,) * (len(shape) - dim - 1))

    gain = one(*cuts[0])
    for cut in cuts[1:]:
        gain = gain * one(*cut)
    return gain


def bell_draw(own_key, shape, scale, reach, pieces=(), kind=jnp.bfloat16):
    values = scale * jax.random.normal(own_key, shape, jnp.float32)
    if pieces:
        values = values * block_scale(own_key, shape, pieces, -0.22, 0.18)
    return jnp.clip(values, -reach, reach).astype(kind)


def setup_inputs(seed: int = 0) -> dict:
    streams_of = jax.random.split(jax.random.key(seed), 6)
    return {
        "right_side": bell_draw(streams_of[0], (R_DEV, N_ROWS, NRHS, BS), 1.0, 6.0, ((1, 64), (2, 4))),
        "lower": bell_draw(streams_of[1], (R_DEV, N_ROWS, NNZ, BS, BS), (2 * BS * NNZ) ** -0.5, 0.1875, ((1, 64), (2, 4))),
        "diag_inv": bell_draw(streams_of[2], (R_DEV, N_ROWS, BS, BS), BS ** -0.5, 0.5, ((1, 64),)),
        "levels": draw_levels(jax.random.fold_in(streams_of[5], 71), 0),
        "columns": draw_columns(jax.random.fold_in(streams_of[5], 71), 0),
    }


def reference(right_side, lower, diag_inv, levels, columns):
    rhs_all = right_side.reshape(NB, NRHS, BS)
    blocks = lower.reshape(NB, NNZ, BS, BS)
    inverses = diag_inv.reshape(NB, BS, BS)
    level_of = levels.reshape(NB)
    column_of = columns.reshape(NB, NNZ)
    order = jnp.argsort(level_of, stable=True).astype(jnp.int32)
    each = NB // LEVELS
    solution = jnp.zeros((NB, NRHS, BS), jnp.bfloat16)
    for level in range(LEVELS):
        picked = order[level * each:(level + 1) * each]
        partial_value = rhs_all[picked].astype(jnp.float32)
        if level > 0:
            known = solution[column_of[picked]].astype(jnp.float32)
            tiles = blocks[picked].astype(jnp.float32)
            partial_value = partial_value - jnp.einsum("rjcb,rjab->rca", known, tiles)
        partial_value = partial_value.astype(jnp.bfloat16).astype(jnp.float32)
        result = jnp.einsum("rcb,rab->rca", partial_value, inverses[picked].astype(jnp.float32))
        solution = solution.at[picked].set(result.astype(jnp.bfloat16))
    return solution.reshape(R_DEV, NB // R_DEV, NRHS, BS)
```

```python
import functools

import jax
import jax.numpy as jnp
from jax import lax
from jax.experimental import pallas as pl
from jax.experimental.pallas import tpu as pltpu
from jax.sharding import PartitionSpec as P

LEVELS = 8
EACH = 2
NNZ = 4
Y, Z, C = 4, 8, 2


def swap(x, mask):
    return lax.ppermute(x, "rows", [(i, i ^ mask) for i in range(Y * Z * C)])


def exchange(x):
    line = jnp.concatenate([x] + [swap(x, d << 1) for d in range(1, Z)], 0)
    plane = jnp.concatenate([line] + [swap(line, e << 4) for e in range(1, Y)], 0)
    return plane, swap(plane, 1)


def level_kernel(level, plan, *refs):
    n_known = 2 * level
    known = refs[:n_known]
    rhs, inverse = refs[n_known : n_known + 2]
    at = n_known + 2
    tiles = None
    if level > 0:
        tiles = refs[at]
        at += 2
    fresh, solved, rhs_buf, inv_buf, out_buf, sems = refs[at : at + 6]
    known_buf, tile_buf, known_sems, tile_sems = refs[at + 6 : at + 10] if level > 0 else (None,) * 4

    rows = [plan[level * EACH + m] for m in range(EACH)]
    first = []
    for m in range(EACH):
        if level > 0:
            for j in range(NNZ):
                s = m * NNZ + j
                code = plan[LEVELS * EACH + (level * EACH + m) * NNZ + j]
                which = code // 256
                place = code % 256
                for k in range(n_known):

                    @pl.when(which == k)
                    def _(k=k, s=s, place=place):
                        pltpu.make_async_copy(known[k].at[place], known_buf.at[s], known_sems.at[s]).start()

            pltpu.make_async_copy(tiles.at[rows[m]], tile_buf.at[m], tile_sems.at[m]).start()
        c1 = pltpu.make_async_copy(rhs.at[rows[m]], rhs_buf.at[m], sems.at[m])
        c2 = pltpu.make_async_copy(inverse.at[rows[m]], inv_buf.at[m], sems.at[EACH + m])
        c1.start()
        c2.start()
        first.append((c1, c2))
    outs = []
    for m in range(EACH):
        first[m][0].wait()
        total = rhs_buf[m].astype(jnp.float32)
        if level > 0:
            pltpu.make_async_copy(tiles.at[rows[m]], tile_buf.at[m], tile_sems.at[m]).wait()
            for j in range(NNZ):
                s = m * NNZ + j
                pltpu.make_async_copy(known[0].at[0], known_buf.at[s], known_sems.at[s]).wait()
                total = total - lax.dot_general(
                    known_buf[s], tile_buf[m, j], (((1,), (1,)), ((), ())), preferred_element_type=jnp.float32
                )
        first[m][1].wait()
        x = lax.dot_general(
            total.astype(jnp.bfloat16), inv_buf[m], (((1,), (1,)), ((), ())), preferred_element_type=jnp.float32
        ).astype(jnp.bfloat16)
        fresh[m] = x
        out_buf[m] = x
        c = pltpu.make_async_copy(out_buf.at[m], solved.at[rows[m]], sems.at[2 * EACH + m])
        c.start()
        outs.append(c)
    for c in outs:
        c.wait()


def solve_level(level, plan, known, rhs, inverse, tiles, solved):
    n, width, block = rhs.shape
    kind = rhs.dtype
    any_spec = pl.BlockSpec(memory_space=pl.ANY)
    operands = [plan, *known, rhs, inverse]
    scratch = [
        pltpu.VMEM((EACH, width, block), kind),
        pltpu.VMEM((EACH, block, block), kind),
        pltpu.VMEM((EACH, width, block), kind),
        pltpu.SemaphoreType.DMA((3 * EACH,)),
    ]
    aliases = {}
    if level > 0:
        operands += [tiles, solved]
        aliases = {len(operands) - 1: 1}
        scratch += [
            pltpu.VMEM((EACH * NNZ, width, block), kind),
            pltpu.VMEM((EACH, NNZ, block, block), kind),
            pltpu.SemaphoreType.DMA((EACH * NNZ,)),
            pltpu.SemaphoreType.DMA((EACH,)),
        ]
    return pl.pallas_call(
        functools.partial(level_kernel, level),
        out_shape=(jax.ShapeDtypeStruct((EACH, width, block), kind), jax.ShapeDtypeStruct(rhs.shape, kind)),
        in_specs=[pl.BlockSpec(memory_space=pltpu.SMEM)] + [any_spec] * (len(operands) - 1),
        out_specs=(pl.BlockSpec(memory_space=pltpu.VMEM), any_spec),
        scratch_shapes=scratch,
        input_output_aliases=aliases,
        name=f"level_{level}",
    )(*operands)


def make_plan(levels, column_of, me):
    n = levels.shape[0]
    row = jnp.arange(n, dtype=jnp.int32)
    earlier = row[None, :] < row[:, None]
    same = levels[:, None, :] == levels[None, :, :]
    rank = jnp.sum(jnp.where(same & earlier[:, :, None], 1, 0), 1)
    spot = levels * EACH + rank
    mine = lax.dynamic_index_in_dim(spot, me, 1, keepdims=False)
    hit = mine[None, :] == row[:, None]
    order = jnp.sum(jnp.where(hit, row[None, :], 0), 1)
    wanted = jnp.sum(jnp.where(hit[:, :, None], column_of[None], 0), 1).reshape(-1)
    everyone = jnp.arange(spot.size, dtype=jnp.int32)
    found = jnp.sum(jnp.where(wanted[:, None] == everyone[None, :], spot.reshape(-1)[None, :], 0), 1)
    apart = (wanted % (Y * Z * C)) ^ me
    code = (found // EACH * C + apart % C) * 256 + apart // C * EACH + found % EACH
    return jnp.concatenate([order, code])


def local(right_side, lower, diag_inv, levels, columns):
    me = lax.axis_index("rows")
    rhs = right_side[:, 0]
    inverse = diag_inv[:, 0]
    plan = make_plan(levels, columns[:, 0], me)
    tiles = lax.all_gather(lower[:, 0], "rhs", axis=1, tiled=True)
    known, solved = [], None
    for level in range(LEVELS):
        fresh, solved = solve_level(level, plan, known, rhs, inverse, tiles, solved)
        if level < LEVELS - 1:
            known += exchange(fresh)
    return solved[:, None]


def solution(mesh):
    in_specs = (
        P(None, "rows", "rhs", None),
        P(None, "rows", "rhs", None, None),
        P(None, "rows", None, None),
        P(),
        P(None, "rows", None),
    )
    out_specs = P(None, "rows", "rhs", None)
    return jax.shard_map(local, mesh=mesh, in_specs=in_specs, out_specs=out_specs, check_vma=False)
```

```python
import functools

import jax
import jax.numpy as jnp
from jax import lax
from jax.experimental import pallas as pl
from jax.experimental.pallas import tpu as pltpu
from jax.sharding import PartitionSpec as P

LEVELS = 8
EACH = 2
NNZ = 4
SLOTS = EACH * NNZ
Y, Z, C = 4, 8, 2
HALF = Z // 2
LINE = HALF * C * EACH
ABSENT = 255
VMEM = pl.BlockSpec(memory_space=pltpu.VMEM)
SMEM = pl.BlockSpec(memory_space=pltpu.SMEM)
ANY = pl.BlockSpec(memory_space=pl.ANY)
PARAMS = pltpu.CompilerParams(vmem_limit_bytes=16 * 2**20)


def swap(x, mask):
    return lax.ppermute(x, "rows", [(i, i ^ mask) for i in range(Y * Z * C)])


def line_exchange(x):
    chip = jnp.concatenate([x, swap(x, 1)], 0)
    line = []
    for k in range(HALF):
        pairs = [(i, i ^ ((HALF * (i % C) + k) << 1)) for i in range(Y * Z * C)]
        line.append(lax.ppermute(chip, "rows", pairs))
    half = jnp.concatenate(line, 0)
    return half, swap(half, 1)


def times_transposed(x, w):
    return lax.dot_general(x, w, (((1,), (1,)), ((), ())), preferred_element_type=jnp.float32)


def first_kernel(order, rhs, inverse, fresh, rhs_out, inverse_out, sems):
    n = rhs.shape[0]
    copies = []
    for p in range(n):
        row = order[p]
        copies.append(
            (
                pltpu.make_async_copy(rhs.at[row], rhs_out.at[p], sems.at[p]),
                pltpu.make_async_copy(inverse.at[row], inverse_out.at[p], sems.at[n + p]),
            )
        )
        for c in copies[-1]:
            c.start()
    for m in range(EACH):
        for c in copies[m]:
            c.wait()
        fresh[m] = times_transposed(rhs_out[m], inverse_out[m]).astype(fresh.dtype)
    for pair in copies[EACH:]:
        for c in pair:
            c.wait()


def tiles_kernel(order, tiles, tiles_out, sems):
    copies = [pltpu.make_async_copy(tiles.at[order[p]], tiles_out.at[p], sems.at[p]) for p in range(tiles.shape[0])]
    for c in copies:
        c.start()
    for c in copies:
        c.wait()


def select_kernel(level, codes, half, other, *refs):
    store, *messages = refs[-(1 + Y) :]
    store[2 * level - 2] = half[...]
    store[2 * level - 1] = other[...]
    for e in range(Y):
        for s in range(SLOTS):
            code = codes[(e * LEVELS + level) * SLOTS + s]

            @pl.when(code // LINE < 2 * level)
            def _(e=e, s=s, code=code):
                messages[e][s] = store[code // LINE, code % LINE]


def level_kernel(level, codes, order, rhs, inverse, tiles, *refs):
    messages = refs[:Y]
    out = refs[-1]
    for m in range(EACH):
        p = level * EACH + m
        total = rhs[p].astype(jnp.float32)
        for j in range(NNZ):
            s = m * NNZ + j
            source = codes[(Y * LEVELS + level) * SLOTS + s]
            known = messages[0][s]
            for e in range(1, Y):
                known = jnp.where(source == e, messages[e][s], known)
            total = total - times_transposed(known, tiles[p, j])
        x = times_transposed(total.astype(jnp.bfloat16), inverse[p]).astype(jnp.bfloat16)
        if level < LEVELS - 1:
            out[m] = x
        else:
            out[order[p]] = x
    if level == LEVELS - 1:
        for k, earlier in enumerate(refs[Y:-1]):
            for m in range(EACH):
                out[order[k * EACH + m]] = earlier[m]


def spots_of(levels):
    row = jnp.arange(levels.shape[0], dtype=jnp.int32)
    earlier = row[None, :] < row[:, None]
    same = levels[:, None, :] == levels[None, :, :]
    return levels * EACH + jnp.sum(jnp.where(same & earlier[:, :, None], 1, 0), 1)


def make_codes(spot, columns, me):
    n, count = spot.shape
    row = jnp.arange(n, dtype=jnp.int32)
    people = me ^ (jnp.arange(Y, dtype=jnp.int32) * (Z * C))
    theirs = jnp.sum(
        jnp.where(people[:, None, None] == jnp.arange(count, dtype=jnp.int32)[None, None, :], spot[None], 0), 2
    )
    hit = theirs[:, None, :] == row[None, :, None]
    wanted = jnp.sum(jnp.where(hit[:, :, :, None], columns[:, None], 0), 2).reshape(-1)
    everyone = jnp.arange(spot.size, dtype=jnp.int32)
    found = jnp.sum(jnp.where(wanted[:, None] == everyone[None, :], spot.reshape(-1)[None, :], 0), 1)
    apart = (wanted % count) ^ me
    y_apart, z_apart, core_apart = apart // (Z * C), apart // C % Z, apart % C
    other = (z_apart // HALF) ^ (me % C)
    place = ((z_apart % HALF) * C + (core_apart ^ other)) * EACH + found % EACH
    code = (found // EACH * 2 + other) * LINE + place
    code = jnp.where(y_apart == 0, code, ABSENT * LINE)
    return jnp.concatenate([code, y_apart[: n * NNZ]])


def local(right_side, lower, diag_inv, levels, columns):
    me = lax.axis_index("rows")
    rhs, inverse, mine = right_side[:, 0], diag_inv[:, 0], columns[:, 0]
    n, width, block = rhs.shape
    kind = rhs.dtype
    shape = jax.ShapeDtypeStruct
    tiles = lax.all_gather(lower[:, 0], "rhs", axis=1, tiled=True)
    all_columns = jnp.stack([mine] + [swap(mine, e * Z * C) for e in range(1, Y)], 0)
    spot = spots_of(levels)
    own = lax.dynamic_index_in_dim(spot, me, 1, keepdims=False)
    row = jnp.arange(n, dtype=jnp.int32)
    order = jnp.sum(jnp.where(own[None, :] == row[:, None], row[None, :], 0), 1)
    codes = make_codes(spot, all_columns, me)

    fresh, rhs, inverse = pl.pallas_call(
        first_kernel,
        out_shape=(shape((EACH, width, block), kind), shape(rhs.shape, kind), shape(inverse.shape, kind)),
        in_specs=[SMEM, ANY, ANY],
        out_specs=(VMEM, VMEM, VMEM),
        scratch_shapes=[pltpu.SemaphoreType.DMA((2 * n,))],
        compiler_params=PARAMS,
        name="first",
    )(order, rhs, inverse)
    tiles = pl.pallas_call(
        tiles_kernel,
        out_shape=shape(tiles.shape, kind),
        in_specs=[SMEM, ANY],
        out_specs=VMEM,
        scratch_shapes=[pltpu.SemaphoreType.DMA((n,))],
        compiler_params=PARAMS,
        name="tiles",
    )(order, tiles)
    solved = [fresh]
    store = None
    for level in range(1, LEVELS):
        half, other = line_exchange(fresh)
        store_shape = shape((2 * (LEVELS - 1), LINE, width, block), kind)
        store, *messages = pl.pallas_call(
            functools.partial(select_kernel, level),
            out_shape=(store_shape,) + (shape((SLOTS, width, block), kind),) * Y,
            in_specs=[SMEM, VMEM, VMEM] + [VMEM] * (level > 1),
            out_specs=(VMEM,) * (1 + Y),
            input_output_aliases={3: 0} if level > 1 else {},
            compiler_params=PARAMS,
            name=f"select_{level}",
        )(codes, half, other, *([store] if level > 1 else []))
        messages = messages[:1] + [swap(messages[e], e * Z * C) for e in range(1, Y)]
        last = level == LEVELS - 1
        operands = [codes, order, rhs, inverse, tiles, *messages] + (solved if last else [])
        fresh = pl.pallas_call(
            functools.partial(level_kernel, level),
            out_shape=shape((n if last else EACH, width, block), kind),
            in_specs=[SMEM, SMEM] + [VMEM] * (len(operands) - 2),
            out_specs=VMEM,
            compiler_params=PARAMS,
            name=f"level_{level}",
        )(*operands)
        solved.append(fresh)
    return fresh[:, None]


def solution(mesh):
    in_specs = (
        P(None, "rows", "rhs", None),
        P(None, "rows", "rhs", None, None),
        P(None, "rows", None, None),
        P(),
        P(None, "rows", None),
    )
    out_specs = P(None, "rows", "rhs", None)
    return jax.shard_map(local, mesh=mesh, in_specs=in_specs, out_specs=out_specs, check_vma=False)
```

```python
import functools

import jax
import jax.numpy as jnp
from jax import lax
from jax.experimental import pallas as pl
from jax.experimental.pallas import tpu as pltpu
from jax.sharding import Mesh
from jax.sharding import PartitionSpec as P

LEVELS = 8
EACH = 2
NNZ = 4
SLOTS = EACH * NNZ
Y, Z, C, X = 4, 8, 2, 4
ROWS = ("y", "z", "core")
HALF = Z // 2
LINE = HALF * C * EACH
EARLY = 2
FIRST = EARLY * EACH
LATE = (LEVELS - EARLY) * EACH
SHARE = LATE // X
PLACES = 2 * EARLY * LINE
ABSENT = 255
VMEM = pl.BlockSpec(memory_space=pltpu.VMEM)
SMEM = pl.BlockSpec(memory_space=pltpu.SMEM)
ANY = pl.BlockSpec(memory_space=pl.ANY)
PARAMS = pltpu.CompilerParams(vmem_limit_bytes=24 * 2**20)
shape = jax.ShapeDtypeStruct


def swap(x, mask):
    return lax.ppermute(x, ROWS, [(i, i ^ mask) for i in range(Y * Z * C)])


def swap_y(pieces):
    return pieces[:1] + [swap(pieces[e], e * Z * C) for e in range(1, Y)]


def line_exchange(x):
    chip = jnp.concatenate([x, swap(x, 1)], 0)
    line = []
    for k in range(HALF):
        pairs = [(i, i ^ ((HALF * (i % C) + k) << 1)) for i in range(Y * Z * C)]
        line.append(lax.ppermute(chip, ROWS, pairs))
    half = jnp.concatenate(line, 0)
    return half, swap(half, 1)


def times_transposed(x, w):
    return lax.dot_general(x, w, (((1,), (1,)), ((), ())), preferred_element_type=jnp.float32)


def run_copies(pairs, sems):
    copies = [pltpu.make_async_copy(a, b, sems.at[i]) for i, (a, b) in enumerate(pairs)]
    for c in copies:
        c.start()
    for c in copies:
        c.wait()


def first_kernel(order, rhs, inverse, fresh, rhs_out, inverse_out, sems):
    pairs = [(rhs.at[order[p]], rhs_out.at[p]) for p in range(FIRST)]
    pairs += [(inverse.at[order[p]], inverse_out.at[p]) for p in range(FIRST)]
    run_copies(pairs, sems)
    for m in range(EACH):
        fresh[m] = times_transposed(rhs_out[m], inverse_out[m]).astype(fresh.dtype)


def pack_kernel(order, rhs, tiles, inverse, payload, early, *refs):
    quarters, (buf, sems) = refs[:Y], refs[Y:]
    n = order.shape[0] - 2
    y, x = order[n], order[n + 1]
    pairs = [(rhs.at[order[FIRST + p]], buf.at[p]) for p in range(LATE)]
    pairs += [(tiles.at[order[EACH + p]], early.at[p]) for p in range(EACH * (EARLY - 1))]
    pairs += [(tiles.at[order[FIRST + p]], payload.at[p]) for p in range(LATE)]
    pairs += [(inverse.at[order[FIRST + SHARE * x + p]], payload.at[LATE + p]) for p in range(SHARE)]
    run_copies(pairs, sems)
    part = quarters[0].shape[1]
    for e in range(Y):
        quarters[e][...] = buf[:, pl.ds(pl.multiple_of((y ^ e) * part, part), part), :]


def select_kernel(codes, half, other, *messages):
    kept = (half, other)
    for e in range(Y):
        for s in range(SLOTS):
            code = codes[e * SLOTS + s]
            for o in range(2):

                @pl.when(code // LINE == o)
                def _(e=e, s=s, o=o, code=code):
                    messages[e][s] = kept[o][code % LINE]


def early_kernel(codes, order, rhs, inverse, tiles, *refs):
    messages, out = refs[:Y], refs[Y]
    x = order[order.shape[0] - 1]
    for m in range(EACH):
        total = rhs[EACH + m].astype(jnp.float32)
        for j in range(NNZ):
            s = m * NNZ + j
            source = codes[Y * SLOTS + s]
            known = messages[0][s]
            for e in range(1, Y):
                known = jnp.where(source == e, messages[e][s], known)
            total = total - times_transposed(known, tiles[x ^ j, m])
        out[m] = times_transposed(total.astype(jnp.bfloat16), inverse[EACH + m]).astype(out.dtype)


def split_kernel(order, *refs):
    kept, messages = refs[: 2 * EARLY], refs[2 * EARLY :]
    y = order[order.shape[0] - 2]
    part = messages[0].shape[1]
    for e in range(Y):
        columns = pl.ds(pl.multiple_of((y ^ e) * part, part), part)
        for i, k in enumerate(kept):
            messages[e][i * LINE : (i + 1) * LINE] = k[:, columns, :]


def late_kernel(level, codes, order, factor, *refs):
    rhs, refs = refs[:Y], refs[Y:]
    last = level == LEVELS - 1
    n_new = Y if level == EARLY else 2
    new, refs = refs[:n_new], refs[n_new:]
    if level > EARLY:
        refs = refs[1:]
    solved, refs = (refs[: level - EARLY], refs[level - EARLY :]) if last else ([], refs)
    store, outs = refs[0], refs[1:]
    start = 0 if level == EARLY else Y + 2 * (level - 1 - EARLY)
    for i, piece in enumerate(new):
        store[start + i] = piece[...]
    y = order[order.shape[0] - 2]
    for e in range(Y):
        for m in range(EACH):
            p = (level - EARLY) * EACH + m
            total = rhs[e][p].astype(jnp.float32)
            for j in range(NNZ):
                code = codes[(e * LATE + p) * NNZ + j]
                known = store[code // PLACES, code % PLACES]
                total = total - times_transposed(known, factor[(y ^ e) * X + j, p])
            inverse = factor[(y ^ e) * X + p // SHARE, LATE + p % SHARE]
            x = times_transposed(total.astype(jnp.bfloat16), inverse).astype(jnp.bfloat16)
            if last:
                outs[e][p] = x
            else:
                outs[0][e * EACH + m] = x
    for k, piece in enumerate(solved):
        for e in range(Y):
            outs[e][k * EACH : (k + 1) * EACH] = piece[e * EACH : (e + 1) * EACH]


def gather_kernel(order, *refs):
    early, pieces, out = refs[:EARLY], refs[EARLY : EARLY + Y], refs[-1]
    y = order[order.shape[0] - 2]
    part = pieces[0].shape[1]
    for k in range(EARLY):
        for m in range(EACH):
            out[order[k * EACH + m]] = early[k][m]
    for p in range(LATE):
        for e in range(Y):
            out[order[FIRST + p], pl.ds(pl.multiple_of((y ^ e) * part, part), part), :] = pieces[e][p]


def spots_of(levels):
    row = jnp.arange(levels.shape[0], dtype=jnp.int32)
    earlier = row[None, :] < row[:, None]
    same = levels[:, None, :] == levels[None, :, :]
    return levels * EACH + jnp.sum(jnp.where(same & earlier[:, :, None], 1, 0), 1)


def make_codes(spot, columns, me):
    n, count = spot.shape
    row = jnp.arange(n, dtype=jnp.int32)
    people = me ^ (jnp.arange(Y, dtype=jnp.int32) * (Z * C))
    theirs = jnp.sum(
        jnp.where(people[:, None, None] == jnp.arange(count, dtype=jnp.int32)[None, None, :], spot[None], 0), 2
    )
    hit = theirs[:, None, :] == row[None, :, None]
    wanted = jnp.sum(jnp.where(hit[:, :, :, None], columns[:, None], 0), 2)
    wanted = wanted.reshape(-1)
    everyone = jnp.arange(spot.size, dtype=jnp.int32)
    found = jnp.sum(jnp.where(wanted[:, None] == everyone[None, :], spot.reshape(-1)[None, :], 0), 1)
    apart = (wanted % count) ^ me
    y_apart, z_apart, core_apart = apart // (Z * C), apart // C % Z, apart % C
    other = (z_apart // HALF) ^ (me % C)
    chip = (z_apart % HALF) * C + (core_apart ^ other)
    level, member = found // EACH, found % EACH
    line = other * LINE + chip * EACH + member
    early = jnp.where(y_apart == 0, line, ABSENT * LINE).reshape(Y, n * NNZ)
    first = slice(EACH * NNZ, FIRST * NNZ)
    early = jnp.concatenate([early[:, first].reshape(-1), y_apart[first]])
    late = jnp.where(
        level < EARLY,
        y_apart * PLACES + level * (2 * LINE) + line,
        (Y + 2 * (level - EARLY) + other) * PLACES + (chip * Y + y_apart) * EACH + member,
    )
    return early, late.reshape(Y, n * NNZ)[:, FIRST * NNZ :].reshape(-1)


def local(right_side, lower, diag_inv, levels, columns):
    me = lax.axis_index(ROWS)
    my_x = lax.axis_index("rhs")
    rhs, inverse, own_tiles, mine = right_side[:, 0], diag_inv[:, 0], lower[:, 0, 0], columns[:, 0]
    n, width, block = rhs.shape
    part = width // Y
    kind = rhs.dtype

    def call(kernel, out, specs, operands, name, out_specs=None, **more):
        return pl.pallas_call(
            kernel,
            out_shape=out,
            in_specs=specs,
            out_specs=out_specs or ((VMEM,) * len(out) if isinstance(out, tuple) else VMEM),
            compiler_params=PARAMS,
            name=name,
            **more,
        )(*operands)

    spot = spots_of(levels)
    own = lax.dynamic_index_in_dim(spot, me, 1, keepdims=False)
    row = jnp.arange(n, dtype=jnp.int32)
    order = jnp.sum(jnp.where(own[None, :] == row[:, None], row[None, :], 0), 1)
    order = jnp.concatenate([order, jnp.stack([me // (Z * C), my_x]).astype(jnp.int32)])

    quarter = shape((LATE, part, block), kind)
    n_copies = 2 * LATE + EACH * (EARLY - 1) + SHARE
    payload, early_tiles, *quarters = call(
        pack_kernel,
        (shape((LATE + SHARE, block, block), kind), shape((EACH * (EARLY - 1), block, block), kind)) + (quarter,) * Y,
        [SMEM, ANY, ANY, ANY],
        (order, rhs, own_tiles, inverse),
        "pack",
        out_specs=(ANY,) + (VMEM,) * (1 + Y),
        scratch_shapes=[pltpu.VMEM((LATE, width, block), kind), pltpu.SemaphoreType.DMA((n_copies,))],
    )
    factor = lax.all_gather(payload, ("y", "rhs"), axis=0)
    fresh, rhs_early, inverse_early = call(
        first_kernel,
        (shape((EACH, width, block), kind), shape((FIRST, width, block), kind), shape((FIRST, block, block), kind)),
        [SMEM, ANY, ANY],
        (order, rhs, inverse),
        "first",
        scratch_shapes=[pltpu.SemaphoreType.DMA((2 * FIRST,))],
    )
    tiles = jnp.stack(
        [early_tiles] + [lax.ppermute(early_tiles, "rhs", [(i, i ^ k) for i in range(X)]) for k in range(1, X)], 0
    )
    all_columns = jnp.stack([mine] + [swap(mine, e * Z * C) for e in range(1, Y)], 0)
    codes, late_codes = make_codes(spot, all_columns, me)
    solved = [fresh]

    kept = list(line_exchange(fresh))
    messages = call(select_kernel, (shape((SLOTS, width, block), kind),) * Y, [SMEM] + [VMEM] * 2, (codes, *kept), "select")
    messages = swap_y(list(messages))
    fresh = call(
        early_kernel,
        shape((EACH, width, block), kind),
        [SMEM, SMEM] + [VMEM] * (3 + Y),
        (codes, order, rhs_early, inverse_early, tiles, *messages),
        "level_1",
    )
    solved.append(fresh)
    quarters = swap_y(list(quarters))

    kept += line_exchange(fresh)
    new = call(split_kernel, (shape((PLACES, part, block), kind),) * Y, [SMEM] + [VMEM] * 4, (order, *kept), "split")
    new = swap_y(list(new))
    store = []
    late = []
    store_shape = shape((Y + 2 * (LEVELS - 1 - EARLY), PLACES, part, block), kind)
    for level in range(EARLY, LEVELS):
        last = level == LEVELS - 1
        operands = [late_codes, order, factor, *quarters, *new, *store]
        aliases = {len(operands) - 1: 0} if store else {}
        operands += late if last else []
        store, *outs = call(
            functools.partial(late_kernel, level),
            (store_shape,) + ((quarter,) * Y if last else (shape((Y * EACH, part, block), kind),)),
            [SMEM, SMEM] + [VMEM] * (len(operands) - 2),
            operands,
            f"level_{level}",
            input_output_aliases=aliases,
        )
        store = [store]
        if not last:
            late += outs
            new = line_exchange(outs[0])
    pieces = swap_y(outs)
    out = call(gather_kernel, shape(rhs.shape, kind), [SMEM] + [VMEM] * (EARLY + Y), (order, *solved, *pieces), "gather")
    return out[:, None]


def solution(mesh):
    parts = Mesh(mesh.devices.reshape(Y, Z, C, X), ROWS + ("rhs",))
    in_specs = (
        P(None, ROWS, "rhs", None),
        P(None, ROWS, "rhs", None, None),
        P(None, ROWS, None, None),
        P(),
        P(None, ROWS, None),
    )
    out_specs = P(None, ROWS, "rhs", None)
    return jax.shard_map(local, mesh=parts, in_specs=in_specs, out_specs=out_specs, check_vma=False)
```

```python
import functools

import jax
import jax.numpy as jnp
from jax import lax
from jax.experimental import pallas as pl
from jax.experimental.pallas import tpu as pltpu
from jax.sharding import Mesh
from jax.sharding import PartitionSpec as P

LEVELS = 8
EACH = 2
NNZ = 4
SLOTS = EACH * NNZ
Y, Z, C, X = 4, 8, 2, 4
ROWS = ("y", "z", "core")
HALF = Z // 2
LINE = HALF * C * EACH
EARLY = 2
FIRST = EARLY * EACH
LATE = (LEVELS - EARLY) * EACH
GROUP = 3
GROUPS = (LEVELS - EARLY) // GROUP
SHARE = -(-GROUP * EACH // X)
PLACES = HALF * C * Y * EACH
BASE = 32
ABSENT = 255
VMEM = pl.BlockSpec(memory_space=pltpu.VMEM)
SMEM = pl.BlockSpec(memory_space=pltpu.SMEM)
ANY = pl.BlockSpec(memory_space=pl.ANY)
PARAMS = pltpu.CompilerParams(vmem_limit_bytes=16 * 2**20)
shape = jax.ShapeDtypeStruct


def swap(x, mask):
    return lax.ppermute(x, ROWS, [(i, i ^ mask) for i in range(Y * Z * C)])


def swap_y(pieces):
    return pieces[:1] + [swap(pieces[e], e * Z * C) for e in range(1, Y)]


def line_exchange(x, after=None, beside=None):
    chip = jnp.concatenate([x, swap(x, 1)], 0)
    if after is not None:
        chip, after = lax.optimization_barrier((chip, after))
    line = []
    for k in range(HALF):
        pairs = [(i, i ^ ((HALF * (i % C) + k) << 1)) for i in range(Y * Z * C)]
        line.append(lax.ppermute(chip, ROWS, pairs))
    half = jnp.concatenate(line, 0)
    if beside is not None:
        half, beside = lax.optimization_barrier((half, beside(after) if after is not None else beside))
    return (half, swap(half, 1)), beside


def times_transposed(x, w):
    return lax.dot_general(x, w, (((1,), (1,)), ((), ())), preferred_element_type=jnp.float32)


def run_copies(pairs, sems):
    copies = [pltpu.make_async_copy(a, b, sems.at[i]) for i, (a, b) in enumerate(pairs)]
    for c in copies:
        c.start()
    for c in copies:
        c.wait()


def quarters_of(order, rows, outs, at=0):
    part = outs[0].shape[1]
    y = order[order.shape[0] - 2]
    for e in range(Y):
        outs[e][at : at + rows.shape[0]] = rows[:, pl.ds(pl.multiple_of((y ^ e) * part, part), part), :]


def first_kernel(order, rhs, inverse, digits, fresh, rhs_early, inverse_early, *refs):
    messages, (rows, factors, sems) = refs[:Y], refs[Y:]
    n = rows.shape[0]
    pairs = [(rhs.at[order[p]], rows.at[p]) for p in range(n)]
    pairs += [(inverse.at[order[p]], factors.at[p]) for p in range(FIRST)]
    run_copies(pairs, sems)
    for m in range(EACH):
        fresh[m] = times_transposed(rows[m], factors[m]).astype(fresh.dtype)
    rhs_early[...] = rows[EACH:FIRST]
    inverse_early[...] = factors[EACH:FIRST]
    quarters_of(order, rows.at[FIRST:], messages)
    for e in range(Y):
        messages[e][LATE] = digits[...]


def pack_kernel(order, tiles, inverse, early, *refs):
    payloads, sems = refs[:-1], refs[-1]
    x = order[order.shape[0] - 1]
    rows = GROUP * EACH
    pairs = [(tiles.at[order[EACH + p]], early.at[p]) for p in range(EACH)]
    for g, payload in enumerate(payloads):
        start = FIRST + g * rows
        pairs += [(tiles.at[order[start + p]], payload.at[p]) for p in range(rows)]
        for p in range(SHARE):
            pairs.append((inverse.at[order[start + jnp.minimum(SHARE * x + p, rows - 1)]], payload.at[rows + p]))
    run_copies(pairs, sems)


def select_kernel(codes, half, other, *messages):
    kept = (half, other)
    for e in range(Y):
        for s in range(SLOTS):
            code = codes[e * SLOTS + s]
            for o in range(2):

                @pl.when(code // LINE == o)
                def _(e=e, s=s, o=o, code=code):
                    messages[e][s] = kept[o][code % LINE]


def early_kernel(codes, order, rhs, inverse, tiles, *refs):
    messages, out, outs = refs[:Y], refs[Y], refs[Y + 1 :]
    x = order[order.shape[0] - 1]
    for m in range(EACH):
        total = rhs[m].astype(jnp.float32)
        for j in range(NNZ):
            s = m * NNZ + j
            source = codes[Y * SLOTS + s]
            known = messages[0][s]
            for e in range(1, Y):
                known = jnp.where(source == e, messages[e][s], known)
            total = total - times_transposed(known, tiles[x ^ j, m])
        out[m] = times_transposed(total.astype(jnp.bfloat16), inverse[m]).astype(out.dtype)
    quarters_of(order, out, outs)


def split_kernel(order, half, other, *messages):
    quarters_of(order, half, messages)
    quarters_of(order, other, messages, LINE)


def late_kernel(level, codes, order, factor, *refs):
    n = order.shape[0] - 2
    last = level == LEVELS - 1
    rhs, new, refs = refs[:Y], refs[Y : Y + 2], refs[Y + 2 :]
    if level == EARLY:
        oldest, refs = refs[:Y], refs[Y:]
    else:
        oldest, refs = (), refs[1:]
    solved, refs = (refs[: level - EARLY], refs[level - EARLY :]) if last else ([], refs)
    store, outs = refs[0], refs[1:]
    for e, piece in enumerate(oldest):
        at = e * 2 * LINE
        store[at // PLACES, at % PLACES : at % PLACES + 2 * LINE] = piece[...]
    for i, piece in enumerate(new):
        store[2 * (level - 1) + i] = piece[...]
    y = order[n]
    for e in range(Y):
        for m in range(EACH):
            p = (level - EARLY) * EACH + m
            q = p % (GROUP * EACH)
            total = rhs[e][p].astype(jnp.float32)
            for j in range(NNZ):
                code = codes[(e * LATE + p) * NNZ + j]
                known = store[code // PLACES, code % PLACES]
                total = total - times_transposed(known, factor[(y ^ e) * X + j, q])
            inverse = factor[(y ^ e) * X + q // SHARE, GROUP * EACH + q % SHARE]
            x = times_transposed(total.astype(jnp.bfloat16), inverse).astype(jnp.bfloat16)
            if last:
                outs[e][p] = x
            else:
                outs[0][e * EACH + m] = x
    for k, piece in enumerate(solved):
        for e in range(Y):
            outs[e][k * EACH : (k + 1) * EACH] = piece[e * EACH : (e + 1) * EACH]


def gather_kernel(order, *refs):
    early, pieces, out = refs[:EARLY], refs[EARLY : EARLY + Y], refs[-1]
    y = order[order.shape[0] - 2]
    part = pieces[0].shape[1]
    for k in range(EARLY):
        for m in range(EACH):
            out[order[k * EACH + m]] = early[k][m]
    for p in range(LATE):
        for e in range(Y):
            out[order[FIRST + p], pl.ds(pl.multiple_of((y ^ e) * part, part), part), :] = pieces[e][p]


def spots_of(levels):
    row = jnp.arange(levels.shape[0], dtype=jnp.int32)
    earlier = row[None, :] < row[:, None]
    same = levels[:, None, :] == levels[None, :, :]
    return levels * EACH + jnp.sum(jnp.where(same & earlier[:, :, None], 1, 0), 1)


def make_codes(spot, columns, me):
    n, count = spot.shape
    row = jnp.arange(n, dtype=jnp.int32)
    people = me ^ (jnp.arange(Y, dtype=jnp.int32) * (Z * C))
    theirs = jnp.sum(
        jnp.where(people[:, None, None] == jnp.arange(count, dtype=jnp.int32)[None, None, :], spot[None], 0), 2
    )
    hit = theirs[:, None, :] == row[None, :, None]
    wanted = jnp.sum(jnp.where(hit[:, :, :, None], columns[:, None], 0), 2)
    wanted = wanted.reshape(-1)
    everyone = jnp.arange(spot.size, dtype=jnp.int32)
    found = jnp.sum(jnp.where(wanted[:, None] == everyone[None, :], spot.reshape(-1)[None, :], 0), 1)
    apart = (wanted % count) ^ me
    y_apart, z_apart, core_apart = apart // (Z * C), apart // C % Z, apart % C
    other = (z_apart // HALF) ^ (me % C)
    chip = (z_apart % HALF) * C + (core_apart ^ other)
    level, member = found // EACH, found % EACH
    line = other * LINE + chip * EACH + member
    early = jnp.where(y_apart == 0, line, ABSENT * LINE).reshape(Y, n * NNZ)
    first = slice(EACH * NNZ, FIRST * NNZ)
    early = jnp.concatenate([early[:, first].reshape(-1), y_apart[first]])
    late = jnp.where(
        level == 0,
        y_apart * (2 * LINE) + line,
        (2 * level + other) * PLACES + (chip * Y + y_apart) * EACH + member,
    )
    return early, late.reshape(Y, n * NNZ)[:, FIRST * NNZ :].reshape(-1)


def local(right_side, lower, diag_inv, levels, columns):
    me = lax.axis_index(ROWS)
    my_x = lax.axis_index("rhs")
    rhs, inverse, own_tiles, mine = right_side[:, 0], diag_inv[:, 0], lower[:, 0, 0], columns[:, 0]
    n, width, block = rhs.shape
    part = width // Y
    kind = rhs.dtype

    def call(kernel, out, specs, operands, name, out_specs=None, **more):
        return pl.pallas_call(
            kernel,
            out_shape=out,
            in_specs=specs,
            out_specs=out_specs or ((VMEM,) * len(out) if isinstance(out, tuple) else VMEM),
            compiler_params=PARAMS,
            name=name,
            **more,
        )(*operands)

    spot = spots_of(levels)
    own = lax.dynamic_index_in_dim(spot, me, 1, keepdims=False)
    row = jnp.arange(n, dtype=jnp.int32)
    order = jnp.sum(jnp.where(own[None, :] == row[:, None], row[None, :], 0), 1)
    order = jnp.concatenate([order, jnp.stack([me // (Z * C), my_x]).astype(jnp.int32)])

    digits = jnp.concatenate([mine // BASE, mine % BASE], 1).astype(kind)
    digits = jnp.pad(digits, ((0, part - n), (0, block - 2 * NNZ)))

    payload = shape((GROUP * EACH + SHARE, block, block), kind)
    early_tiles, *payloads = pl.pallas_call(
        pack_kernel,
        out_shape=(shape((EACH, block, block), kind),) + (payload,) * GROUPS,
        in_specs=[SMEM, ANY, ANY],
        out_specs=(VMEM,) * (1 + GROUPS),
        scratch_shapes=[pltpu.SemaphoreType.DMA((EACH + GROUPS * (GROUP * EACH + SHARE),))],
        name="pack",
    )(order, own_tiles, inverse)
    factors = [lax.all_gather(p, ("y", "rhs"), axis=0) for p in payloads]
    fresh, rhs_early, inverse_early, *messages = pl.pallas_call(
        first_kernel,
        out_shape=(
            shape((EACH, width, block), kind),
            shape((EACH, width, block), kind),
            shape((EACH, block, block), kind),
        )
        + (shape((LATE + 1, part, block), kind),) * Y,
        in_specs=[SMEM, ANY, ANY, VMEM],
        out_specs=(VMEM,) * (3 + Y),
        scratch_shapes=[
            pltpu.VMEM((n, width, block), kind),
            pltpu.VMEM((FIRST, block, block), kind),
            pltpu.SemaphoreType.DMA((n + FIRST,)),
        ],
        name="first",
    )(order, rhs, inverse, digits)
    def spread(held):
        tiles, messages = held
        over_x = [lax.ppermute(tiles, "rhs", [(i, i ^ k) for i in range(X)]) for k in range(1, X)]
        return jnp.stack([tiles] + over_x, 0), swap_y(list(messages))

    solved = [fresh]
    kept, (tiles, messages) = line_exchange(fresh, (early_tiles, messages), spread)
    read = jnp.stack([m[LATE, :n, : 2 * NNZ] for m in messages], 0).astype(jnp.int32)
    codes, late_codes = make_codes(spot, read[:, :, :NNZ] * BASE + read[:, :, NNZ:], me)
    chosen = call(select_kernel, (shape((SLOTS, width, block), kind),) * Y, [SMEM] + [VMEM] * 2, (codes, *kept), "select")
    chosen = swap_y(list(chosen))
    fresh, *split = call(
        early_kernel,
        (shape((EACH, width, block), kind),) + (shape((EACH, part, block), kind),) * Y,
        [SMEM, SMEM] + [VMEM] * (3 + Y),
        (codes, order, rhs_early, inverse_early, tiles, *chosen),
        "level_1",
    )
    solved.append(fresh)
    oldest = call(split_kernel, (shape((2 * LINE, part, block), kind),) * Y, [SMEM] + [VMEM] * 2, (order, *kept), "split")
    new, oldest = line_exchange(jnp.concatenate(swap_y(list(split)), 0), None, swap_y(list(oldest)))
    store = []
    late = []
    store_shape = shape((2 * (LEVELS - 1), PLACES, part, block), kind)
    for level in range(EARLY, LEVELS):
        last = level == LEVELS - 1
        operands = [late_codes, order, factors[(level - EARLY) // GROUP], *messages, *new, *(store or oldest)]
        aliases = {len(operands) - 1: 0} if store else {}
        operands += late if last else []
        store, *outs = call(
            functools.partial(late_kernel, level),
            (store_shape,) + ((shape((LATE, part, block), kind),) * Y if last else (shape((Y * EACH, part, block), kind),)),
            [SMEM, SMEM] + [VMEM] * (len(operands) - 2),
            operands,
            f"level_{level}",
            input_output_aliases=aliases,
        )
        store = [store]
        if not last:
            late += outs
            new, _ = line_exchange(outs[0])
    pieces = swap_y(outs)
    out = call(gather_kernel, shape(rhs.shape, kind), [SMEM] + [VMEM] * (EARLY + Y), (order, *solved, *pieces), "gather")
    return out[:, None]


def solution(mesh):
    parts = Mesh(mesh.devices.reshape(Y, Z, C, X), ROWS + ("rhs",))
    in_specs = (
        P(None, ROWS, "rhs", None),
        P(None, ROWS, "rhs", None, None),
        P(None, ROWS, None, None),
        P(),
        P(None, ROWS, None),
    )
    out_specs = P(None, ROWS, "rhs", None)
    return jax.shard_map(local, mesh=parts, in_specs=in_specs, out_specs=out_specs, check_vma=False)
```

```python
import functools

import jax
import jax.numpy as jnp
from jax import lax
from jax.experimental import pallas as pl
from jax.experimental.pallas import tpu as pltpu
from jax.sharding import Mesh
from jax.sharding import PartitionSpec as P

LEVELS = 8
EACH = 2
NNZ = 4
SLOTS = EACH * NNZ
Y, Z, C, X = 4, 8, 2, 4
ROWS = ("y", "z", "core")
HALF = Z // 2
LINE = HALF * C * EACH
EARLY = 2
FIRST = EARLY * EACH
LATE = (LEVELS - EARLY) * EACH
GROUP = 3
GROUPS = (LEVELS - EARLY) // GROUP
SHARE = -(-GROUP * EACH // X)
PLACES = HALF * C * Y * EACH
BASE = 32
ABSENT = 255
VMEM = pl.BlockSpec(memory_space=pltpu.VMEM)
SMEM = pl.BlockSpec(memory_space=pltpu.SMEM)
ANY = pl.BlockSpec(memory_space=pl.ANY)
PARAMS = pltpu.CompilerParams(vmem_limit_bytes=16 * 2**20)
shape = jax.ShapeDtypeStruct


def swap(x, mask):
    return lax.ppermute(x, ROWS, [(i, i ^ mask) for i in range(Y * Z * C)])


def swap_y(pieces):
    return pieces[:1] + [swap(pieces[e], e * Z * C) for e in range(1, Y)]


def line_exchange(x, after=None, beside=None):
    chip = jnp.concatenate([x, swap(x, 1)], 0)
    if after is not None:
        chip, after = lax.optimization_barrier((chip, after))
    line = []
    for k in range(HALF):
        pairs = [(i, i ^ ((HALF * (i % C) + k) << 1)) for i in range(Y * Z * C)]
        line.append(lax.ppermute(chip, ROWS, pairs))
    half = jnp.concatenate(line, 0)
    if beside is not None:
        half, beside = lax.optimization_barrier((half, beside(after) if after is not None else beside))
    return (half, swap(half, 1)), beside


def times_transposed(x, w):
    return lax.dot_general(x, w, (((1,), (1,)), ((), ())), preferred_element_type=jnp.float32)


def run_copies(pairs, sems):
    copies = [pltpu.make_async_copy(a, b, sems.at[i]) for i, (a, b) in enumerate(pairs)]
    for c in copies:
        c.start()
    for c in copies:
        c.wait()


def quarters_of(order, rows, outs, at=0):
    part = outs[0].shape[1]
    y = order[order.shape[0] - 2]
    for e in range(Y):
        outs[e][at : at + rows.shape[0]] = rows[:, pl.ds(pl.multiple_of((y ^ e) * part, part), part), :]


def start_kernel(order, rhs, tiles, inverse, fresh, late_rows, rhs_early, inverse_early, early, *refs):
    payloads, (buf, factors, sems) = refs[:GROUPS], refs[GROUPS:]
    x = order[order.shape[0] - 1]
    rows = GROUP * EACH
    pairs = [(rhs.at[order[m]], buf.at[m]) for m in range(EACH)]
    pairs += [(inverse.at[order[m]], factors.at[m]) for m in range(EACH)]
    pairs += [(rhs.at[order[EACH + m]], rhs_early.at[m]) for m in range(EACH)]
    pairs += [(inverse.at[order[EACH + m]], inverse_early.at[m]) for m in range(EACH)]
    pairs += [(rhs.at[order[FIRST + p]], late_rows.at[p]) for p in range(LATE)]
    pairs += [(tiles.at[order[EACH + p]], early.at[p]) for p in range(EACH)]
    for g, payload in enumerate(payloads):
        start = FIRST + g * rows
        pairs += [(tiles.at[order[start + p]], payload.at[p]) for p in range(rows)]
        for p in range(SHARE):
            pairs.append((inverse.at[order[start + jnp.minimum(SHARE * x + p, rows - 1)]], payload.at[rows + p]))
    run_copies(pairs, sems)
    for m in range(EACH):
        fresh[m] = times_transposed(buf[m], factors[m]).astype(fresh.dtype)


def quarter_kernel(order, rows, rhs, inverse, digits, rhs_early, inverse_early, *messages):
    rhs_early[...] = rhs[...]
    inverse_early[...] = inverse[...]
    quarters_of(order, rows, messages)
    for e in range(Y):
        messages[e][LATE] = digits[...]


def select_kernel(codes, half, other, *messages):
    kept = (half, other)
    for e in range(Y):
        for s in range(SLOTS):
            code = codes[e * SLOTS + s]
            for o in range(2):

                @pl.when(code // LINE == o)
                def _(e=e, s=s, o=o, code=code):
                    messages[e][s] = kept[o][code % LINE]


def early_kernel(codes, order, rhs, inverse, tiles, *refs):
    messages, out, outs = refs[:Y], refs[Y], refs[Y + 1 :]
    x = order[order.shape[0] - 1]
    for m in range(EACH):
        total = rhs[m].astype(jnp.float32)
        for j in range(NNZ):
            s = m * NNZ + j
            source = codes[Y * SLOTS + s]
            known = messages[0][s]
            for e in range(1, Y):
                known = jnp.where(source == e, messages[e][s], known)
            total = total - times_transposed(known, tiles[x ^ j, m])
        out[m] = times_transposed(total.astype(jnp.bfloat16), inverse[m]).astype(out.dtype)
    quarters_of(order, out, outs)


def split_kernel(order, half, other, *messages):
    quarters_of(order, half, messages)
    quarters_of(order, other, messages, LINE)


def late_kernel(level, codes, order, factor, *refs):
    n = order.shape[0] - 2
    last = level == LEVELS - 1
    n_lines = 2 * (level - 1)
    rhs, oldest, lines, refs = refs[:Y], refs[Y : 2 * Y], refs[2 * Y : 2 * Y + n_lines], refs[2 * Y + n_lines :]
    solved, refs = (refs[: level - EARLY], refs[level - EARLY :]) if last else ([], refs)
    outs, store = refs[:-1], refs[-1]
    for e, piece in enumerate(oldest):
        at = e * 2 * LINE
        store[at // PLACES, at % PLACES : at % PLACES + 2 * LINE] = piece[...]
    for i, piece in enumerate(lines):
        store[2 + i] = piece[...]
    y = order[n]
    for e in range(Y):
        for m in range(EACH):
            p = (level - EARLY) * EACH + m
            q = p % (GROUP * EACH)
            at = [codes[(e * LATE + p) * NNZ + j] for j in range(NNZ)]
            known = jnp.concatenate([store[k // PLACES, k % PLACES] for k in at], 1)
            tiles = jnp.concatenate([factor[(y ^ e) * X + j, q] for j in range(NNZ)], 1)
            total = rhs[e][p].astype(jnp.float32) - times_transposed(known, tiles)
            inverse = factor[(y ^ e) * X + q // SHARE, GROUP * EACH + q % SHARE]
            x = times_transposed(total.astype(jnp.bfloat16), inverse).astype(jnp.bfloat16)
            if last:
                outs[e][p] = x
            else:
                outs[0][e * EACH + m] = x
    for k, piece in enumerate(solved):
        for e in range(Y):
            outs[e][k * EACH : (k + 1) * EACH] = piece[e * EACH : (e + 1) * EACH]


def gather_kernel(order, *refs):
    early, pieces, out = refs[:EARLY], refs[EARLY : EARLY + Y], refs[-1]
    y = order[order.shape[0] - 2]
    part = pieces[0].shape[1]
    for k in range(EARLY):
        for m in range(EACH):
            out[order[k * EACH + m]] = early[k][m]
    for p in range(LATE):
        for e in range(Y):
            out[order[FIRST + p], pl.ds(pl.multiple_of((y ^ e) * part, part), part), :] = pieces[e][p]


def spots_of(levels):
    row = jnp.arange(levels.shape[0], dtype=jnp.int32)
    earlier = row[None, :] < row[:, None]
    same = levels[:, None, :] == levels[None, :, :]
    return levels * EACH + jnp.sum(jnp.where(same & earlier[:, :, None], 1, 0), 1)


def make_codes(spot, columns, me):
    n, count = spot.shape
    row = jnp.arange(n, dtype=jnp.int32)
    people = me ^ (jnp.arange(Y, dtype=jnp.int32) * (Z * C))
    theirs = jnp.sum(
        jnp.where(people[:, None, None] == jnp.arange(count, dtype=jnp.int32)[None, None, :], spot[None], 0), 2
    )
    hit = theirs[:, None, :] == row[None, :, None]
    wanted = jnp.sum(jnp.where(hit[:, :, :, None], columns[:, None], 0), 2)
    wanted = wanted.reshape(-1)
    everyone = jnp.arange(spot.size, dtype=jnp.int32)
    found = jnp.sum(jnp.where(wanted[:, None] == everyone[None, :], spot.reshape(-1)[None, :], 0), 1)
    apart = (wanted % count) ^ me
    y_apart, z_apart, core_apart = apart // (Z * C), apart // C % Z, apart % C
    other = (z_apart // HALF) ^ (me % C)
    chip = (z_apart % HALF) * C + (core_apart ^ other)
    level, member = found // EACH, found % EACH
    line = other * LINE + chip * EACH + member
    early = jnp.where(y_apart == 0, line, ABSENT * LINE).reshape(Y, n * NNZ)
    first = slice(EACH * NNZ, FIRST * NNZ)
    early = jnp.concatenate([early[:, first].reshape(-1), y_apart[first]])
    late = jnp.where(
        level == 0,
        y_apart * (2 * LINE) + line,
        (2 * level + other) * PLACES + (chip * Y + y_apart) * EACH + member,
    )
    return early, late.reshape(Y, n * NNZ)[:, FIRST * NNZ :].reshape(-1)


def local(right_side, lower, diag_inv, levels, columns):
    me = lax.axis_index(ROWS)
    my_x = lax.axis_index("rhs")
    rhs, inverse, own_tiles, mine = right_side[:, 0], diag_inv[:, 0], lower[:, 0, 0], columns[:, 0]
    n, width, block = rhs.shape
    part = width // Y
    kind = rhs.dtype

    def call(kernel, out, specs, operands, name, out_specs=None, **more):
        return pl.pallas_call(
            kernel,
            out_shape=out,
            in_specs=specs,
            out_specs=out_specs or ((VMEM,) * len(out) if isinstance(out, tuple) else VMEM),
            compiler_params=PARAMS,
            name=name,
            **more,
        )(*operands)

    spot = spots_of(levels)
    own = lax.dynamic_index_in_dim(spot, me, 1, keepdims=False)
    row = jnp.arange(n, dtype=jnp.int32)
    order = jnp.sum(jnp.where(own[None, :] == row[:, None], row[None, :], 0), 1)
    order = jnp.concatenate([order, jnp.stack([me // (Z * C), my_x]).astype(jnp.int32)])

    digits = jnp.concatenate([mine // BASE, mine % BASE], 1).astype(kind)
    digits = jnp.pad(digits, ((0, part - n), (0, block - 2 * NNZ)))

    payload = shape((GROUP * EACH + SHARE, block, block), kind)
    pair = shape((EACH, width, block), kind)
    square = shape((EACH, block, block), kind)
    n_copies = 2 * FIRST + LATE + EACH + GROUPS * (GROUP * EACH + SHARE)
    fresh, late_rows, rhs_early, inverse_early, early_tiles, *payloads = pl.pallas_call(
        start_kernel,
        out_shape=(pair, shape((LATE, width, block), kind), pair, square, square) + (payload,) * GROUPS,
        in_specs=[SMEM, ANY, ANY, ANY],
        out_specs=(VMEM,) * (5 + GROUPS),
        scratch_shapes=[
            pltpu.VMEM((EACH, width, block), kind),
            pltpu.VMEM((EACH, block, block), kind),
            pltpu.SemaphoreType.DMA((n_copies,)),
        ],
        name="start",
    )(order, rhs, own_tiles, inverse)
    factors = [lax.all_gather(p, ("y", "rhs"), axis=0) for p in payloads]

    def spread(held):
        tiles, rows = held
        rhs_now, inverse_now, *messages = call(
            quarter_kernel,
            (pair, square) + (shape((LATE + 1, part, block), kind),) * Y,
            [SMEM] + [VMEM] * 4,
            (order, rows, rhs_early, inverse_early, digits),
            "quarters",
        )
        over_x = [lax.ppermute(tiles, "rhs", [(i, i ^ k) for i in range(X)]) for k in range(1, X)]
        return jnp.stack([tiles] + over_x, 0), swap_y(list(messages)), rhs_now, inverse_now

    solved = [fresh]
    kept, (tiles, messages, rhs_early, inverse_early) = line_exchange(fresh, (early_tiles, late_rows), spread)
    read = jnp.stack([m[LATE, :n, : 2 * NNZ] for m in messages], 0).astype(jnp.int32)
    codes, late_codes = make_codes(spot, read[:, :, :NNZ] * BASE + read[:, :, NNZ:], me)
    chosen = call(select_kernel, (shape((SLOTS, width, block), kind),) * Y, [SMEM] + [VMEM] * 2, (codes, *kept), "select")
    chosen = swap_y(list(chosen))
    fresh, *split = call(
        early_kernel,
        (shape((EACH, width, block), kind),) + (shape((EACH, part, block), kind),) * Y,
        [SMEM, SMEM] + [VMEM] * (3 + Y),
        (codes, order, rhs_early, inverse_early, tiles, *chosen),
        "level_1",
    )
    solved.append(fresh)
    oldest = call(split_kernel, (shape((2 * LINE, part, block), kind),) * Y, [SMEM] + [VMEM] * 2, (order, *kept), "split")
    lines, (oldest, factors[0]) = line_exchange(
        jnp.concatenate(swap_y(list(split)), 0), None, (swap_y(list(oldest)), factors[0])
    )
    lines = list(lines)
    late = []
    for level in range(EARLY, LEVELS):
        last = level == LEVELS - 1
        group = (level - EARLY) // GROUP
        operands = [late_codes, order, factors[group], *messages, *oldest, *lines] + (late if last else [])
        outs = call(
            functools.partial(late_kernel, level),
            (shape((LATE, part, block), kind),) * Y if last else (shape((Y * EACH, part, block), kind),),
            [SMEM, SMEM] + [VMEM] * (len(operands) - 2),
            operands,
            f"level_{level}",
            scratch_shapes=[pltpu.VMEM((2 * level, PLACES, part, block), kind)],
        )
        if not last:
            late += outs
            ends = (level + 1 - EARLY) // GROUP != group
            new, held = line_exchange(outs[0], None, factors[group + 1] if ends else None)
            if ends:
                factors[group + 1] = held
            lines += new
    pieces = swap_y(list(outs))
    out = call(gather_kernel, shape(rhs.shape, kind), [SMEM] + [VMEM] * (EARLY + Y), (order, *solved, *pieces), "gather")
    return out[:, None]


def solution(mesh):
    parts = Mesh(mesh.devices.reshape(Y, Z, C, X), ROWS + ("rhs",))
    in_specs = (
        P(None, ROWS, "rhs", None),
        P(None, ROWS, "rhs", None, None),
        P(None, ROWS, None, None),
        P(),
        P(None, ROWS, None),
    )
    out_specs = P(None, ROWS, "rhs", None)
    return jax.shard_map(local, mesh=parts, in_specs=in_specs, out_specs=out_specs, check_vma=False)
```

```python
import functools

import jax
import jax.numpy as jnp
from jax import lax
from jax.experimental import pallas as pl
from jax.experimental.pallas import tpu as pltpu
from jax.sharding import Mesh
from jax.sharding import PartitionSpec as P

LEVELS = 8
EACH = 2
NNZ = 4
SLOTS = EACH * NNZ
Y, Z, C, X = 4, 8, 2, 4
ROWS = ("y", "z", "core")
HALF = Z // 2
LINE = HALF * C * EACH
EARLY = 2
FIRST = EARLY * EACH
LATE = (LEVELS - EARLY) * EACH
GROUP = 3
GROUPS = (LEVELS - EARLY) // GROUP
SHARE = -(-GROUP * EACH // X)
PLACES = HALF * C * Y * EACH
BASE = 32
ABSENT = 255
VMEM = pl.BlockSpec(memory_space=pltpu.VMEM)
SMEM = pl.BlockSpec(memory_space=pltpu.SMEM)
ANY = pl.BlockSpec(memory_space=pl.ANY)
PARAMS = pltpu.CompilerParams(vmem_limit_bytes=16 * 2**20)
shape = jax.ShapeDtypeStruct


def swap(x, mask):
    return lax.ppermute(x, ROWS, [(i, i ^ mask) for i in range(Y * Z * C)])


def swap_y(pieces):
    return pieces[:1] + [swap(pieces[e], e * Z * C) for e in range(1, Y)]


def line_exchange(x, after=None, beside=None):
    chip = jnp.concatenate([x, swap(x, 1)], 0)
    if after is not None:
        chip, after = lax.optimization_barrier((chip, after))
    line = []
    for k in range(HALF):
        far = HALF + (HALF - k) % HALF
        pairs = [(i, i ^ ((far if i % C else k) << 1)) for i in range(Y * Z * C)]
        line.append(lax.ppermute(chip, ROWS, pairs))
    half = jnp.concatenate(line, 0)
    if beside is not None:
        half, beside = lax.optimization_barrier((half, beside(after) if after is not None else beside))
    return (half, swap(half, 1)), beside


def times_transposed(x, w):
    return lax.dot_general(x, w, (((1,), (1,)), ((), ())), preferred_element_type=jnp.float32)


def run_copies(pairs, sems):
    copies = [pltpu.make_async_copy(a, b, sems.at[i]) for i, (a, b) in enumerate(pairs)]
    for c in copies:
        c.start()
    for c in copies:
        c.wait()


def quarters_of(order, rows, outs, at=0):
    part = outs[0].shape[1]
    y = order[order.shape[0] - 2]
    for e in range(Y):
        outs[e][at : at + rows.shape[0]] = rows[:, pl.ds(pl.multiple_of((y ^ e) * part, part), part), :]


def start_kernel(order, rhs, tiles, inverse, fresh, late_rows, rhs_early, inverse_early, early, *refs):
    payloads, (buf, factors, sems) = refs[:GROUPS], refs[GROUPS:]
    x = order[order.shape[0] - 1]
    rows = GROUP * EACH
    pairs = [(rhs.at[order[m]], buf.at[m]) for m in range(EACH)]
    pairs += [(inverse.at[order[m]], factors.at[m]) for m in range(EACH)]
    pairs += [(rhs.at[order[EACH + m]], rhs_early.at[m]) for m in range(EACH)]
    pairs += [(inverse.at[order[EACH + m]], inverse_early.at[m]) for m in range(EACH)]
    pairs += [(rhs.at[order[FIRST + p]], late_rows.at[p]) for p in range(LATE)]
    pairs += [(tiles.at[order[EACH + p]], early.at[p]) for p in range(EACH)]
    for g, payload in enumerate(payloads):
        start = FIRST + g * rows
        pairs += [(tiles.at[order[start + p]], payload.at[p]) for p in range(rows)]
        for p in range(SHARE):
            pairs.append((inverse.at[order[start + jnp.minimum(SHARE * x + p, rows - 1)]], payload.at[rows + p]))
    run_copies(pairs, sems)
    for m in range(EACH):
        fresh[m] = times_transposed(buf[m], factors[m]).astype(fresh.dtype)


def quarter_kernel(order, rows, rhs, inverse, digits, rhs_early, inverse_early, *messages):
    rhs_early[...] = rhs[...]
    inverse_early[...] = inverse[...]
    quarters_of(order, rows, messages)
    for e in range(Y):
        messages[e][LATE] = digits[...]


def select_kernel(codes, half, other, *messages):
    kept = (half, other)
    for e in range(Y):
        for s in range(SLOTS):
            code = codes[e * SLOTS + s]
            for o in range(2):

                @pl.when(code // LINE == o)
                def _(e=e, s=s, o=o, code=code):
                    messages[e][s] = kept[o][code % LINE]


def early_kernel(codes, order, rhs, inverse, tiles, *refs):
    messages, out, outs = refs[:Y], refs[Y], refs[Y + 1 :]
    x = order[order.shape[0] - 1]
    for m in range(EACH):
        total = rhs[m].astype(jnp.float32)
        for j in range(NNZ):
            s = m * NNZ + j
            source = codes[Y * SLOTS + s]
            known = messages[0][s]
            for e in range(1, Y):
                known = jnp.where(source == e, messages[e][s], known)
            total = total - times_transposed(known, tiles[x ^ j, m])
        out[m] = times_transposed(total.astype(jnp.bfloat16), inverse[m]).astype(out.dtype)
    quarters_of(order, out, outs)


def split_kernel(order, half, other, *messages):
    quarters_of(order, half, messages)
    quarters_of(order, other, messages, LINE)


def late_kernel(level, codes, order, factor, *refs):
    n = order.shape[0] - 2
    last = level == LEVELS - 1
    n_lines = 2 * (level - 1)
    rhs, oldest, lines, refs = refs[:Y], refs[Y : 2 * Y], refs[2 * Y : 2 * Y + n_lines], refs[2 * Y + n_lines :]
    solved, refs = (refs[: level - EARLY], refs[level - EARLY :]) if last else ([], refs)
    outs, store = refs[:-1], refs[-1]
    for e, piece in enumerate(oldest):
        at = e * 2 * LINE
        store[at // PLACES, at % PLACES : at % PLACES + 2 * LINE] = piece[...]
    for i, piece in enumerate(lines):
        store[2 + i] = piece[...]
    y = order[n]
    for e in range(Y):
        for m in range(EACH):
            p = (level - EARLY) * EACH + m
            q = p % (GROUP * EACH)
            at = [codes[(e * LATE + p) * NNZ + j] for j in range(NNZ)]
            known = jnp.concatenate([store[k // PLACES, k % PLACES] for k in at], 1)
            tiles = jnp.concatenate([factor[(y ^ e) * X + j, q] for j in range(NNZ)], 1)
            total = rhs[e][p].astype(jnp.float32) - times_transposed(known, tiles)
            inverse = factor[(y ^ e) * X + q // SHARE, GROUP * EACH + q % SHARE]
            x = times_transposed(total.astype(jnp.bfloat16), inverse).astype(jnp.bfloat16)
            if last:
                outs[e][p] = x
            else:
                outs[0][e * EACH + m] = x
    for k, piece in enumerate(solved):
        for e in range(Y):
            outs[e][k * EACH : (k + 1) * EACH] = piece[e * EACH : (e + 1) * EACH]


def gather_kernel(order, *refs):
    early, pieces, out = refs[:EARLY], refs[EARLY : EARLY + Y], refs[-1]
    y = order[order.shape[0] - 2]
    part = pieces[0].shape[1]
    for k in range(EARLY):
        for m in range(EACH):
            out[order[k * EACH + m]] = early[k][m]
    for p in range(LATE):
        for e in range(Y):
            out[order[FIRST + p], pl.ds(pl.multiple_of((y ^ e) * part, part), part), :] = pieces[e][p]


def spots_of(levels):
    row = jnp.arange(levels.shape[0], dtype=jnp.int32)
    earlier = row[None, :] < row[:, None]
    same = levels[:, None, :] == levels[None, :, :]
    return levels * EACH + jnp.sum(jnp.where(same & earlier[:, :, None], 1, 0), 1)


def make_codes(spot, columns, me):
    n, count = spot.shape
    row = jnp.arange(n, dtype=jnp.int32)
    people = me ^ (jnp.arange(Y, dtype=jnp.int32) * (Z * C))
    theirs = jnp.sum(
        jnp.where(people[:, None, None] == jnp.arange(count, dtype=jnp.int32)[None, None, :], spot[None], 0), 2
    )
    hit = theirs[:, None, :] == row[None, :, None]
    wanted = jnp.sum(jnp.where(hit[:, :, :, None], columns[:, None], 0), 2)
    wanted = wanted.reshape(-1)
    everyone = jnp.arange(spot.size, dtype=jnp.int32)
    found = jnp.sum(jnp.where(wanted[:, None] == everyone[None, :], spot.reshape(-1)[None, :], 0), 1)
    apart = (wanted % count) ^ me
    y_apart, z_apart, core_apart = apart // (Z * C), apart // C % Z, apart % C
    other = (z_apart // HALF) ^ (me % C)
    turn = jnp.where(z_apart < HALF, z_apart, (Z - z_apart) % HALF)
    chip = turn * C + (core_apart ^ other)
    level, member = found // EACH, found % EACH
    line = other * LINE + chip * EACH + member
    early = jnp.where(y_apart == 0, line, ABSENT * LINE).reshape(Y, n * NNZ)
    first = slice(EACH * NNZ, FIRST * NNZ)
    early = jnp.concatenate([early[:, first].reshape(-1), y_apart[first]])
    late = jnp.where(
        level == 0,
        y_apart * (2 * LINE) + line,
        (2 * level + other) * PLACES + (chip * Y + y_apart) * EACH + member,
    )
    return early, late.reshape(Y, n * NNZ)[:, FIRST * NNZ :].reshape(-1)


def local(right_side, lower, diag_inv, levels, columns):
    me = lax.axis_index(ROWS)
    my_x = lax.axis_index("rhs")
    rhs, inverse, own_tiles, mine = right_side[:, 0], diag_inv[:, 0], lower[:, 0, 0], columns[:, 0]
    n, width, block = rhs.shape
    part = width // Y
    kind = rhs.dtype

    def call(kernel, out, specs, operands, name, out_specs=None, **more):
        return pl.pallas_call(
            kernel,
            out_shape=out,
            in_specs=specs,
            out_specs=out_specs or ((VMEM,) * len(out) if isinstance(out, tuple) else VMEM),
            compiler_params=PARAMS,
            name=name,
            **more,
        )(*operands)

    spot = spots_of(levels)
    own = lax.dynamic_index_in_dim(spot, me, 1, keepdims=False)
    row = jnp.arange(n, dtype=jnp.int32)
    order = jnp.sum(jnp.where(own[None, :] == row[:, None], row[None, :], 0), 1)
    order = jnp.concatenate([order, jnp.stack([me // (Z * C), my_x]).astype(jnp.int32)])

    digits = jnp.concatenate([mine // BASE, mine % BASE], 1).astype(kind)
    digits = jnp.pad(digits, ((0, part - n), (0, block - 2 * NNZ)))

    payload = shape((GROUP * EACH + SHARE, block, block), kind)
    pair = shape((EACH, width, block), kind)
    square = shape((EACH, block, block), kind)
    n_copies = 2 * FIRST + LATE + EACH + GROUPS * (GROUP * EACH + SHARE)
    fresh, late_rows, rhs_early, inverse_early, early_tiles, *payloads = pl.pallas_call(
        start_kernel,
        out_shape=(pair, shape((LATE, width, block), kind), pair, square, square) + (payload,) * GROUPS,
        in_specs=[SMEM, ANY, ANY, ANY],
        out_specs=(VMEM,) * (5 + GROUPS),
        scratch_shapes=[
            pltpu.VMEM((EACH, width, block), kind),
            pltpu.VMEM((EACH, block, block), kind),
            pltpu.SemaphoreType.DMA((n_copies,)),
        ],
        name="start",
    )(order, rhs, own_tiles, inverse)
    factors = [lax.all_gather(p, ("y", "rhs"), axis=0) for p in payloads]

    def spread(held):
        tiles, rows = held
        rhs_now, inverse_now, *messages = call(
            quarter_kernel,
            (pair, square) + (shape((LATE + 1, part, block), kind),) * Y,
            [SMEM] + [VMEM] * 4,
            (order, rows, rhs_early, inverse_early, digits),
            "quarters",
        )
        over_x = [lax.ppermute(tiles, "rhs", [(i, i ^ k) for i in range(X)]) for k in range(1, X)]
        return jnp.stack([tiles] + over_x, 0), swap_y(list(messages)), rhs_now, inverse_now

    solved = [fresh]
    kept, (tiles, messages, rhs_early, inverse_early) = line_exchange(fresh, (early_tiles, late_rows), spread)
    read = jnp.stack([m[LATE, :n, : 2 * NNZ] for m in messages], 0).astype(jnp.int32)
    codes, late_codes = make_codes(spot, read[:, :, :NNZ] * BASE + read[:, :, NNZ:], me)
    chosen = call(select_kernel, (shape((SLOTS, width, block), kind),) * Y, [SMEM] + [VMEM] * 2, (codes, *kept), "select")
    chosen = swap_y(list(chosen))
    fresh, *split = call(
        early_kernel,
        (shape((EACH, width, block), kind),) + (shape((EACH, part, block), kind),) * Y,
        [SMEM, SMEM] + [VMEM] * (3 + Y),
        (codes, order, rhs_early, inverse_early, tiles, *chosen),
        "level_1",
    )
    solved.append(fresh)
    oldest = call(split_kernel, (shape((2 * LINE, part, block), kind),) * Y, [SMEM] + [VMEM] * 2, (order, *kept), "split")
    lines, (oldest, factors[0]) = line_exchange(
        jnp.concatenate(swap_y(list(split)), 0), None, (swap_y(list(oldest)), factors[0])
    )
    lines = list(lines)
    late = []
    for level in range(EARLY, LEVELS):
        last = level == LEVELS - 1
        group = (level - EARLY) // GROUP
        operands = [late_codes, order, factors[group], *messages, *oldest, *lines] + (late if last else [])
        outs = call(
            functools.partial(late_kernel, level),
            (shape((LATE, part, block), kind),) * Y if last else (shape((Y * EACH, part, block), kind),),
            [SMEM, SMEM] + [VMEM] * (len(operands) - 2),
            operands,
            f"level_{level}",
            scratch_shapes=[pltpu.VMEM((2 * level, PLACES, part, block), kind)],
        )
        if not last:
            late += outs
            ends = (level + 1 - EARLY) // GROUP != group
            new, held = line_exchange(outs[0], None, factors[group + 1] if ends else None)
            if ends:
                factors[group + 1] = held
            lines += new
    pieces = swap_y(list(outs))
    out = call(gather_kernel, shape(rhs.shape, kind), [SMEM] + [VMEM] * (EARLY + Y), (order, *solved, *pieces), "gather")
    return out[:, None]


def solution(mesh):
    parts = Mesh(mesh.devices.reshape(Y, Z, C, X), ROWS + ("rhs",))
    in_specs = (
        P(None, ROWS, "rhs", None),
        P(None, ROWS, "rhs", None, None),
        P(None, ROWS, None, None),
        P(),
        P(None, ROWS, None),
    )
    out_specs = P(None, ROWS, "rhs", None)
    return jax.shard_map(local, mesh=parts, in_specs=in_specs, out_specs=out_specs, check_vma=False)
```

```python
import functools

import jax
import jax.numpy as jnp
from jax import lax
from jax.experimental import pallas as pl
from jax.experimental.pallas import tpu as pltpu
from jax.sharding import Mesh
from jax.sharding import PartitionSpec as P

LEVELS = 8
EACH = 2
NNZ = 4
SLOTS = EACH * NNZ
Y, Z, C, X = 4, 8, 2, 4
ROWS = ("y", "z", "core")
HALF = Z // 2
LINE = HALF * C * EACH
EARLY = 2
FIRST = EARLY * EACH
LATE = (LEVELS - EARLY) * EACH
GROUP = 3
GROUPS = (LEVELS - EARLY) // GROUP
SHARE = -(-GROUP * EACH // X)
PLACES = HALF * C * Y * EACH
BASE = 32
ABSENT = 255
VMEM = pl.BlockSpec(memory_space=pltpu.VMEM)
SMEM = pl.BlockSpec(memory_space=pltpu.SMEM)
ANY = pl.BlockSpec(memory_space=pl.ANY)
PARAMS = pltpu.CompilerParams(vmem_limit_bytes=16 * 2**20)
shape = jax.ShapeDtypeStruct


def swap(x, mask):
    return lax.ppermute(x, ROWS, [(i, i ^ mask) for i in range(Y * Z * C)])


def swap_y(pieces):
    return pieces[:1] + [swap(pieces[e], e * Z * C) for e in range(1, Y)]


def line_exchange(x, after=None, beside=None):
    chip = jnp.concatenate([x, swap(x, 1)], 0)
    if after is not None:
        chip, after = lax.optimization_barrier((chip, after))
    line = []
    for k in range(HALF):
        pairs = [(i, i ^ ((HALF * (i % C) + k) << 1)) for i in range(Y * Z * C)]
        line.append(lax.ppermute(chip, ROWS, pairs))
    half = jnp.concatenate(line, 0)
    if beside is not None:
        half, beside = lax.optimization_barrier((half, beside(after) if after is not None else beside))
    return (half, swap(half, 1)), beside


def times_transposed(x, w):
    return lax.dot_general(x, w, (((1,), (1,)), ((), ())), preferred_element_type=jnp.float32)


def run_copies(pairs, sems):
    copies = [pltpu.make_async_copy(a, b, sems.at[i]) for i, (a, b) in enumerate(pairs)]
    for c in copies:
        c.start()
    for c in copies:
        c.wait()


def quarters_of(order, rows, outs, at=0):
    part = outs[0].shape[1]
    y = order[order.shape[0] - 2]
    for e in range(Y):
        outs[e][at : at + rows.shape[0]] = rows[:, pl.ds(pl.multiple_of((y ^ e) * part, part), part), :]


def start_kernel(order, rhs, tiles, inverse, fresh, late_rows, rhs_early, inverse_early, early, *refs):
    payloads, (buf, factors, sems) = refs[:GROUPS], refs[GROUPS:]
    x = order[order.shape[0] - 1]
    rows = GROUP * EACH
    pairs = [(rhs.at[order[m]], buf.at[m]) for m in range(EACH)]
    pairs += [(inverse.at[order[m]], factors.at[m]) for m in range(EACH)]
    pairs += [(rhs.at[order[EACH + m]], rhs_early.at[m]) for m in range(EACH)]
    pairs += [(inverse.at[order[EACH + m]], inverse_early.at[m]) for m in range(EACH)]
    pairs += [(rhs.at[order[FIRST + p]], late_rows.at[p]) for p in range(LATE)]
    pairs += [(tiles.at[order[EACH + p]], early.at[p]) for p in range(EACH)]
    for g, payload in enumerate(payloads):
        start = FIRST + g * rows
        pairs += [(tiles.at[order[start + p]], payload.at[p]) for p in range(rows)]
        for p in range(SHARE):
            pairs.append((inverse.at[order[start + jnp.minimum(SHARE * x + p, rows - 1)]], payload.at[rows + p]))
    run_copies(pairs, sems)
    for m in range(EACH):
        fresh[m] = times_transposed(buf[m], factors[m]).astype(fresh.dtype)


def quarter_kernel(order, rows, rhs, inverse, digits, rhs_early, inverse_early, *messages):
    rhs_early[...] = rhs[...]
    inverse_early[...] = inverse[...]
    quarters_of(order, rows, messages)
    for e in range(Y):
        messages[e][LATE] = digits[...]


def select_kernel(codes, half, other, *messages):
    kept = (half, other)
    for e in range(Y):
        for s in range(SLOTS):
            code = codes[e * SLOTS + s]
            for o in range(2):

                @pl.when(code // LINE == o)
                def _(e=e, s=s, o=o, code=code):
                    messages[e][s] = kept[o][code % LINE]


def early_kernel(codes, order, rhs, inverse, tiles, *refs):
    messages, out, outs = refs[:Y], refs[Y], refs[Y + 1 :]
    x = order[order.shape[0] - 1]
    for m in range(EACH):
        total = rhs[m].astype(jnp.float32)
        for j in range(NNZ):
            s = m * NNZ + j
            source = codes[Y * SLOTS + s]
            known = messages[0][s]
            for e in range(1, Y):
                known = jnp.where(source == e, messages[e][s], known)
            total = total - times_transposed(known, tiles[x ^ j, m])
        out[m] = times_transposed(total.astype(jnp.bfloat16), inverse[m]).astype(out.dtype)
    quarters_of(order, out, outs)


def split_kernel(order, half, other, *messages):
    quarters_of(order, half, messages)
    quarters_of(order, other, messages, LINE)


def late_kernel(level, codes, order, factor, *refs):
    n = order.shape[0] - 2
    last = level == LEVELS - 1
    n_lines = 2 * (level - 1)
    rhs, oldest, lines, refs = refs[:Y], refs[Y : 2 * Y], refs[2 * Y : 2 * Y + n_lines], refs[2 * Y + n_lines :]
    solved, refs = (refs[: level - EARLY], refs[level - EARLY :]) if last else ([], refs)
    outs, store = refs[:-1], refs[-1]
    for e, piece in enumerate(oldest):
        at = e * 2 * LINE
        store[at // PLACES, at % PLACES : at % PLACES + 2 * LINE] = piece[...]
    for i, piece in enumerate(lines):
        store[2 + i] = piece[...]
    y = order[n]
    for e in range(Y):
        for m in range(EACH):
            p = (level - EARLY) * EACH + m
            q = p % (GROUP * EACH)
            at = [codes[(e * LATE + p) * NNZ + j] for j in range(NNZ)]
            known = jnp.concatenate([store[k // PLACES, k % PLACES] for k in at], 1)
            tiles = jnp.concatenate([factor[(y ^ e) * X + j, q] for j in range(NNZ)], 1)
            total = rhs[e][p].astype(jnp.float32) - times_transposed(known, tiles)
            inverse = factor[(y ^ e) * X + q // SHARE, GROUP * EACH + q % SHARE]
            x = times_transposed(total.astype(jnp.bfloat16), inverse).astype(jnp.bfloat16)
            if last:
                outs[e][p] = x
            else:
                outs[0][e * EACH + m] = x
    for k, piece in enumerate(solved):
        for e in range(Y):
            outs[e][k * EACH : (k + 1) * EACH] = piece[e * EACH : (e + 1) * EACH]


def gather_kernel(order, *refs):
    early, pieces, out = refs[:EARLY], refs[EARLY : EARLY + Y], refs[-1]
    y = order[order.shape[0] - 2]
    part = pieces[0].shape[1]
    for k in range(EARLY):
        for m in range(EACH):
            out[order[k * EACH + m]] = early[k][m]
    for p in range(LATE):
        for e in range(Y):
            out[order[FIRST + p], pl.ds(pl.multiple_of((y ^ e) * part, part), part), :] = pieces[e][p]


def spots_of(levels):
    row = jnp.arange(levels.shape[0], dtype=jnp.int32)
    earlier = row[None, :] < row[:, None]
    same = levels[:, None, :] == levels[None, :, :]
    return levels * EACH + jnp.sum(jnp.where(same & earlier[:, :, None], 1, 0), 1)


def make_codes(spot, columns, me):
    n, count = spot.shape
    row = jnp.arange(n, dtype=jnp.int32)
    people = me ^ (jnp.arange(Y, dtype=jnp.int32) * (Z * C))
    theirs = jnp.sum(
        jnp.where(people[:, None, None] == jnp.arange(count, dtype=jnp.int32)[None, None, :], spot[None], 0), 2
    )
    hit = theirs[:, None, :] == row[None, :, None]
    wanted = jnp.sum(jnp.where(hit[:, :, :, None], columns[:, None], 0), 2)
    wanted = wanted.reshape(-1)
    everyone = jnp.arange(spot.size, dtype=jnp.int32)
    found = jnp.sum(jnp.where(wanted[:, None] == everyone[None, :], spot.reshape(-1)[None, :], 0), 1)
    apart = (wanted % count) ^ me
    y_apart, z_apart, core_apart = apart // (Z * C), apart // C % Z, apart % C
    other = (z_apart // HALF) ^ (me % C)
    chip = (z_apart % HALF) * C + (core_apart ^ other)
    level, member = found // EACH, found % EACH
    line = other * LINE + chip * EACH + member
    early = jnp.where(y_apart == 0, line, ABSENT * LINE).reshape(Y, n * NNZ)
    first = slice(EACH * NNZ, FIRST * NNZ)
    early = jnp.concatenate([early[:, first].reshape(-1), y_apart[first]])
    late = jnp.where(
        level == 0,
        y_apart * (2 * LINE) + line,
        (2 * level + other) * PLACES + (chip * Y + y_apart) * EACH + member,
    )
    return early, late.reshape(Y, n * NNZ)[:, FIRST * NNZ :].reshape(-1)


def local(right_side, lower, diag_inv, levels, columns):
    me = lax.axis_index(ROWS)
    my_x = lax.axis_index("rhs")
    rhs, inverse, own_tiles, mine = right_side[:, 0], diag_inv[:, 0], lower[:, 0, 0], columns[:, 0]
    n, width, block = rhs.shape
    part = width // Y
    kind = rhs.dtype

    def call(kernel, out, specs, operands, name, out_specs=None, **more):
        return pl.pallas_call(
            kernel,
            out_shape=out,
            in_specs=specs,
            out_specs=out_specs or ((VMEM,) * len(out) if isinstance(out, tuple) else VMEM),
            compiler_params=PARAMS,
            name=name,
            **more,
        )(*operands)

    spot = spots_of(levels)
    own = spots_of(lax.dynamic_slice_in_dim(levels, me, 1, 1))[:, 0]
    row = jnp.arange(n, dtype=jnp.int32)
    order = jnp.sum(jnp.where(own[None, :] == row[:, None], row[None, :], 0), 1)
    order = jnp.concatenate([order, jnp.stack([me // (Z * C), my_x]).astype(jnp.int32)])

    digits = jnp.concatenate([mine // BASE, mine % BASE], 1).astype(kind)
    digits = jnp.pad(digits, ((0, part - n), (0, block - 2 * NNZ)))

    payload = shape((GROUP * EACH + SHARE, block, block), kind)
    pair = shape((EACH, width, block), kind)
    square = shape((EACH, block, block), kind)
    n_copies = 2 * FIRST + LATE + EACH + GROUPS * (GROUP * EACH + SHARE)
    fresh, late_rows, rhs_early, inverse_early, early_tiles, *payloads = pl.pallas_call(
        start_kernel,
        out_shape=(pair, shape((LATE, width, block), kind), pair, square, square) + (payload,) * GROUPS,
        in_specs=[SMEM, ANY, ANY, ANY],
        out_specs=(VMEM,) * (5 + GROUPS),
        scratch_shapes=[
            pltpu.VMEM((EACH, width, block), kind),
            pltpu.VMEM((EACH, block, block), kind),
            pltpu.SemaphoreType.DMA((n_copies,)),
        ],
        name="start",
    )(order, rhs, own_tiles, inverse)
    factors = [lax.all_gather(p, ("y", "rhs"), axis=0) for p in payloads]

    def spread(held):
        tiles, rows = held
        rhs_now, inverse_now, *messages = call(
            quarter_kernel,
            (pair, square) + (shape((LATE + 1, part, block), kind),) * Y,
            [SMEM] + [VMEM] * 4,
            (order, rows, rhs_early, inverse_early, digits),
            "quarters",
        )
        over_x = [lax.ppermute(tiles, "rhs", [(i, i ^ k) for i in range(X)]) for k in range(1, X)]
        return jnp.stack([tiles] + over_x, 0), swap_y(list(messages)), rhs_now, inverse_now

    solved = [fresh]
    kept, (tiles, messages, rhs_early, inverse_early) = line_exchange(fresh, (early_tiles, late_rows), spread)
    read = jnp.stack([m[LATE, :n, : 2 * NNZ] for m in messages], 0).astype(jnp.int32)
    codes, late_codes = make_codes(spot, read[:, :, :NNZ] * BASE + read[:, :, NNZ:], me)
    chosen = call(select_kernel, (shape((SLOTS, width, block), kind),) * Y, [SMEM] + [VMEM] * 2, (codes, *kept), "select")
    chosen = swap_y(list(chosen))
    fresh, *split = call(
        early_kernel,
        (shape((EACH, width, block), kind),) + (shape((EACH, part, block), kind),) * Y,
        [SMEM, SMEM] + [VMEM] * (3 + Y),
        (codes, order, rhs_early, inverse_early, tiles, *chosen),
        "level_1",
    )
    solved.append(fresh)
    oldest = call(split_kernel, (shape((2 * LINE, part, block), kind),) * Y, [SMEM] + [VMEM] * 2, (order, *kept), "split")
    lines, (oldest, factors[0]) = line_exchange(
        jnp.concatenate(swap_y(list(split)), 0), None, (swap_y(list(oldest)), factors[0])
    )
    lines = list(lines)
    late = []
    for level in range(EARLY, LEVELS):
        last = level == LEVELS - 1
        group = (level - EARLY) // GROUP
        operands = [late_codes, order, factors[group], *messages, *oldest, *lines] + (late if last else [])
        outs = call(
            functools.partial(late_kernel, level),
            (shape((LATE, part, block), kind),) * Y if last else (shape((Y * EACH, part, block), kind),),
            [SMEM, SMEM] + [VMEM] * (len(operands) - 2),
            operands,
            f"level_{level}",
            scratch_shapes=[pltpu.VMEM((2 * level, PLACES, part, block), kind)],
        )
        if not last:
            late += outs
            ends = (level + 1 - EARLY) // GROUP != group
            new, held = line_exchange(outs[0], None, factors[group + 1] if ends else None)
            if ends:
                factors[group + 1] = held
            lines += new
    pieces = swap_y(list(outs))
    out = call(gather_kernel, shape(rhs.shape, kind), [SMEM] + [VMEM] * (EARLY + Y), (order, *solved, *pieces), "gather")
    return out[:, None]


def solution(mesh):
    parts = Mesh(mesh.devices.reshape(Y, Z, C, X), ROWS + ("rhs",))
    in_specs = (
        P(None, ROWS, "rhs", None),
        P(None, ROWS, "rhs", None, None),
        P(None, ROWS, None, None),
        P(),
        P(None, ROWS, None),
    )
    out_specs = P(None, ROWS, "rhs", None)
    return jax.shard_map(local, mesh=parts, in_specs=in_specs, out_specs=out_specs, check_vma=False)
```
